32 devices in a mesh: dp: 8 (over z, core), tensor: 4 (over y, x).
Axes of the slice: x: 2, y: 2, z: 4, core: 2. Of those that a mesh axis runs over, the one named last changes fastest.
Arguments:
- tokens: bfloat16 [8, 2048, 2048], P('dp', 'tensor'), may hold values from -6 to 6
- in_weight: bfloat16 [3, 2048, 2048], P(None, 'dp', 'tensor'), may hold values from -0.125 to 0.125
- conv_taps: float32 [3, 2048], replicated, may hold values from -3.5 to 3.5
- out_weight: bfloat16 [2048, 2048], P('tensor', 'dp'), may hold values from -0.125 to 0.125
- gate_weight: bfloat16 [2048, 8192], P('dp', 'tensor'), may hold values from -0.125 to 0.125
- up_weight: bfloat16 [2048, 8192], P('dp', 'tensor'), may hold values from -0.125 to 0.125
- down_weight: bfloat16 [8192, 2048], P('tensor', 'dp'), may hold values from -0.125 to 0.125
- norm_gain1: float32 [2048], replicated, may hold values from 0.1 to 1.9
- norm_gain2: float32 [2048], replicated, may hold values from 0.1 to 1.9
- out_grad: bfloat16 [8, 2048, 2048], P('dp', 'tensor'), may hold values from -6 to 6
Outputs:
- block_out: bfloat16 [8, 2048, 2048], P('dp', 'tensor')
- tokens_grad: float32 [8, 2048, 2048], P('dp', 'tensor')
- in_weight_grad: float32 [3, 2048, 2048], P(None, 'dp', 'tensor')
- conv_taps_grad: float32 [3, 2048], replicated
- out_weight_grad: float32 [2048, 2048], P('tensor', 'dp')
- gate_weight_grad: float32 [2048, 8192], P('dp', 'tensor')
- up_weight_grad: float32 [2048, 8192], P('dp', 'tensor')
- down_weight_grad: float32 [8192, 2048], P('tensor', 'dp')
- gain1_grad: float32 [2048], replicated
- gain2_grad: float32 [2048], replicated
The draws below stay inside these ranges and needn't reach their ends.
All inputs are finite; a program needn't handle non-finite values.
Results may differ from the reference program's by a relative error of at most 0.015.
Values may be sent and summed in bfloat16 or wider, within the bound.
No kernel may reach another device: no remote copies, remote signals or barrier semaphores. Data moves between devices by JAX's collectives and lax.ppermute only.
A program may use at most 256 MiB of HBM per device.

```python
import jax
import jax.numpy as jnp
from jax import lax

D = 2048
FF = 8192
CONV = 3
LEN = 2048
SEQS = 8


def level_of(own_key, extent, split, least, top_value):
    def one(dim, parts):
        steps = jax.random.uniform(jax.random.fold_in(jax.random.fold_in(own_key, 6), dim), (parts,), jnp.float32, least / len(split), top_value / len(split))
        return jnp.repeat(jnp.exp(steps), extent[dim] // parts).reshape((-1,) + (1,) * (len(extent) - dim - 1))

    loudness = one(*split[0])
    for cut in split[1:]:
        loudness = loudness * one(*cut)
    return loudness


def gaussian(own_key, extent, deviation, reach, shards=(), held_as=jnp.bfloat16):
    gain = level_of(own_key, extent, shards, -0.22, 0.18) if shards else 1.0
    array = jax.random.normal(own_key, extent, jnp.float32) * deviation * gain
    return jnp.minimum(jnp.maximum(array, -reach), reach).astype(held_as)


def setup_inputs(seed: int = 0) -> dict:
    arg_keys = jax.random.split(jax.random.key(seed), 11)
    return {
        "tokens": gaussian(arg_keys[0], (SEQS, LEN, D), 1.0, 6.0, ((0, 8), (1, 4))),
        "in_weight": gaussian(arg_keys[1], (3, D, D), D ** -0.5, 0.125, ((1, 8), (2, 4))),
        "conv_taps": gaussian(arg_keys[2], (CONV, D), CONV ** -0.5, 3.5, (), jnp.float32),
        "out_weight": gaussian(arg_keys[3], (D, D), D ** -0.5, 0.125, ((0, 4), (1, 8))),
        "gate_weight": gaussian(arg_keys[4], (D, FF), D ** -0.5, 0.125, ((0, 8), (1, 4))),
        "up_weight": gaussian(arg_keys[5], (D, FF), D ** -0.5, 0.125, ((0, 8), (1, 4))),
        "down_weight": gaussian(arg_keys[6], (FF, D), (FF // 4) ** -0.5, 0.125, ((0, 4), (1, 8))),
        "norm_gain1": jnp.clip(1.0 + 0.18 * jax.random.normal(arg_keys[7], (D,), jnp.float32), 0.1, 1.9),
        "norm_gain2": jnp.clip(1.0 + 0.18 * jax.random.normal(arg_keys[8], (D,), jnp.float32), 0.1, 1.9),
        "out_grad": gaussian(arg_keys[9], (SEQS, LEN, D), 1.0, 6.0, ((0, 8), (1, 4))),
    }


@jax.custom_vjp
def low(v):
    return lax.optimization_barrier(v.astype(jnp.bfloat16)).astype(jnp.float32)

@jax.custom_vjp
def low_back(v):
    return v

def low_keep(v):
    return (low(v), None)

def low_pass(kept, grad):
    return (grad,)

def back_keep(v):
    return (v, None)

def back_low(kept, grad):
    return (low(grad),)
low.defvjp(low_keep, low_pass)
low_back.defvjp(back_keep, back_low)
EPS = 1e-05

def rms_scale(values):
    return lax.rsqrt(lax.optimization_barrier(jnp.mean(values * values, axis=-1, keepdims=True)) + EPS)

def matmul(left, right):
    return jnp.dot(left, right, precision=lax.Precision.HIGHEST, preferred_element_type=jnp.float32)

def causal_conv(values, taps):
    padded = jnp.pad(values, ((2, 0), (0, 0)))
    return taps[0] * padded[:-2] + taps[1] * padded[1:-1] + taps[2] * padded[2:]

def forward(hidden, in_weight, conv_taps, out_weight, gate_weight, up_weight, down_weight, norm_gain1, norm_gain2):
    normed = low(hidden * rms_scale(hidden) * norm_gain1)
    projection_rows = low_back(jnp.stack([matmul(normed, in_weight[k]) for k in range(3)]))
    bgate, cgate, xgate = (projection_rows[0], projection_rows[1], projection_rows[2])
    conv = causal_conv(bgate * xgate, conv_taps)
    output_gate = low(cgate * conv)
    branch = low_back(matmul(output_gate, out_weight))
    second = hidden + branch
    normed2 = low(second * rms_scale(second) * norm_gain2)
    gate_rows = low_back(matmul(normed2, gate_weight))
    upward_rows = low_back(matmul(normed2, up_weight))
    activation_rows = low(jax.nn.silu(gate_rows) * upward_rows)
    ffn = low_back(matmul(activation_rows, down_weight))
    return second + ffn

def reference(tokens, in_weight, conv_taps, out_weight, gate_weight, up_weight, down_weight, norm_gain1, norm_gain2, out_grad):
    weights = tuple((w.astype(jnp.float32) for w in (in_weight, conv_taps, out_weight, gate_weight, up_weight, down_weight, norm_gain1, norm_gain2)))
    zeros = tuple((jnp.zeros_like(w) for w in weights))

    def one_sequence(carry, pair):
        sequence, cotangent = pair
        result, pull = jax.vjp(forward, sequence.astype(jnp.float32), *weights)
        grads = pull(cotangent.astype(jnp.float32))
        summed = tuple((a + b for a, b in zip(carry, grads[1:])))
        return (summed, (result.astype(jnp.bfloat16), grads[0]))
    totals, (results, input_grads) = lax.scan(one_sequence, zeros, (tokens, out_grad))
    return (results, input_grads, totals[0], totals[1], totals[2], totals[3], totals[4], totals[5], totals[6], totals[7])
```

```python
import functools
import math

import jax
import jax.numpy as jnp
from jax import lax
from jax.experimental import pallas as pl
from jax.experimental.pallas import tpu as pltpu
from jax.sharding import PartitionSpec as P

EPS = 1e-05
BF = jnp.bfloat16
F32 = jnp.float32
VMEM_LIMIT = 58 * 2**20
COST = 0.2
NN = (((1,), (0,)), ((), ()))
NT = (((1,), (1,)), ((), ()))
TN = (((0,), (0,)), ((), ()))


def dot(a, b, dims):
    return lax.dot_general(a, b, dims, preferred_element_type=F32)


def after(value, *others):
    if not others:
        return value
    return lax.optimization_barrier((value, others))[0]


def first_after(pieces, *others):
    return [after(pieces[0], *others)] + list(pieces[1:])


def rms_scale(values):
    return lax.rsqrt(jnp.mean(values * values, axis=-1, keepdims=True) + EPS)


def norm_back(hidden, scale, gain, grad):
    scaled = gain * grad
    back = scale * scaled - hidden * scale**3 * jnp.mean(scaled * hidden, axis=-1, keepdims=True)
    return back, jnp.sum(grad * hidden * scale, axis=0)


class Square:
    def __init__(self, nt):
        self.nt = nt
        self.t = lax.axis_index("tensor")
        bits = [1 << i for i in range(int(math.log2(nt)))]
        self.orders = (bits, bits[::-1])
        self.lists = []
        for order in self.orders:
            seen = [0]
            for bit in order:
                seen = seen + [r ^ bit for r in seen]
            self.lists.append(seen)

    def flip(self, value, bit):
        return lax.ppermute(value, "tensor", [(t, t ^ bit) for t in range(self.nt)])

    def gather(self, rows, *gates):
        half = rows.shape[0] // 2
        curs = [rows[:half], rows[half:]]
        depth = len(self.orders[0])
        first = None
        for level in range(depth):
            came = [self.flip(c, o[level]) for c, o in zip(curs, self.orders)]
            first = first or came
            if level < depth - 1:
                curs = [after(jnp.concatenate([c, r]), *gates) for c, r in zip(curs, came)]
        return [curs[0], came[0], curs[1], came[1]], first

    def gather_steps(self, rows):
        half = rows.shape[0] // 2
        curs = [rows[:half], rows[half:]]
        depth = len(self.orders[0])
        gates = None
        for level in range(depth):
            came = [self.flip(c, o[level]) for c, o in zip(curs, self.orders)]
            gates = gates or (yield came)
            if level < depth - 1:
                curs = [after(jnp.concatenate([c, r]), *gates) for c, r in zip(curs, came)]
        yield [curs[0], came[0], curs[1], came[1]]

    def begin(self, far):
        return [self.flip(s, o[-1]) for s, o in zip(far, self.orders)]

    def finish(self, near, came, *gates):
        depth = len(self.orders[0])
        sends = came
        for level in range(depth - 1, -1, -1):
            total = [k.astype(F32) + r.astype(F32) for k, r in zip(near, came)]
            if level:
                half = total[0].shape[0] // 2
                near = [v[:half] for v in total]
                sends = [after(v[half:].astype(BF), *gates) for v in total]
                came = [self.flip(s, o[level - 1]) for s, o in zip(sends, self.orders)]
        return jnp.concatenate(total), sends

    def places(self):
        index = {}
        for h, seen in enumerate(self.lists):
            for i, r in enumerate(seen):
                index[r, h] = h * self.nt + i
        tables = [jnp.array([index[r, h] for r in range(self.nt)]) for h in range(2)]
        before, behind = [], []
        for h, seen in enumerate(self.lists):
            for r in seen:
                at = self.t ^ r
                if h == 1:
                    before.append(jnp.int32(index[r, 0]))
                    there = (jnp.minimum(at + 1, self.nt - 1)) ^ self.t
                    behind.append(jnp.where(at == self.nt - 1, -1, tables[0][there]))
                else:
                    behind.append(jnp.int32(index[r, 1]))
                    there = (jnp.maximum(at - 1, 0)) ^ self.t
                    before.append(jnp.where(at == 0, -1, tables[1][there]))
        return jnp.stack([jnp.stack(before), jnp.stack(behind)]).astype(jnp.int32)


def total_of(value, sizes):
    for axis, size in sizes:
        bit = 1
        while bit < size:
            value = value + lax.ppermute(value, axis, [(i, i ^ bit) for i in range(size)])
            bit *= 2
    return value


def call(name, body, grid, ins, outs, args, flops, scratch=(), scalars=(), aliases=None):
    held = lambda spec: pl.BlockSpec(memory_space=pl.ANY) if spec is None else pl.BlockSpec(
        spec[0],
        lambda j, *_: spec[1](j),
        **({"pipeline_mode": pl.Buffered(1)} if len(spec) > 2 and spec[2] == "held" else {}),
    )
    moved = sum(math.prod(a.shape) * a.dtype.itemsize for a in args)
    moved += sum(math.prod(o[2]) * jnp.dtype(o[3]).itemsize for o in outs)
    return pl.pallas_call(
        body,
        grid_spec=pltpu.PrefetchScalarGridSpec(
            num_scalar_prefetch=len(scalars),
            grid=(grid,),
            in_specs=[held(s) for s in ins],
            out_specs=[pl.BlockSpec(o[0], lambda j, *_, o=o: o[1](j)) for o in outs],
            scratch_shapes=list(scratch),
        ),
        out_shape=[jax.ShapeDtypeStruct(o[2], o[3]) for o in outs],
        name=name,
        input_output_aliases=aliases or {},
        compiler_params=pltpu.CompilerParams(vmem_limit_bytes=VMEM_LIMIT),
        cost_estimate=pl.CostEstimate(
            flops=int(flops * COST), bytes_accessed=int(moved * COST), transcendentals=0
        ),
    )(*scalars, *args)


def whole(a):
    return (a.shape, lambda j: (0,) * a.ndim, "held")


def columns(a, tile, start=0):
    return ((a.shape[0], tile), lambda j: (0, start + j))


def new_columns(rows, width, tile, dtype=BF):
    return ((rows, tile), lambda j: (0, j), (rows, width), dtype)


def gate_body(*refs):
    pieces, (gw, uw, act, silu, slope) = refs[:4], refs[4:]
    rows = pieces[0].shape[0]
    for i in range(4):
        at = pl.ds(i * rows, rows)
        gate = dot(pieces[i][...], gw[...], NN)
        up = dot(pieces[i][...], uw[...], NN)
        sig = jax.nn.sigmoid(gate)
        s = gate * sig
        act[at] = (s * up).astype(BF)
        silu[at] = s.astype(BF)
        slope[at] = (up * sig * (1.0 + gate * (1.0 - sig))).astype(BF)


def ffn_gate(pieces, gate, up):
    dim, width = gate.shape
    tokens = 4 * pieces[0].shape[0]
    tile = min(256, width)
    return call(
        "ffn_gate",
        gate_body,
        width // tile,
        [whole(p) for p in pieces] + [columns(gate, tile), columns(up, tile)],
        [new_columns(tokens, width, tile)] * 3,
        [*pieces, gate, up],
        4 * tokens * dim * width,
    )


def ffn_slope_body(*refs):
    pieces, (w, silu, slope, dgate, dup) = refs[:4], refs[4:]
    rows = pieces[0].shape[0]
    for i in range(4):
        at = pl.ds(i * rows, rows)
        dact = dot(pieces[i][...], w[...], NN)
        dgate[at] = (dact * slope[at].astype(F32)).astype(BF)
        dup[at] = (dact * silu[at].astype(F32)).astype(BF)


def ffn_slope(pieces, down, silu, slope):
    dim, width = down.shape
    tokens = 4 * pieces[0].shape[0]
    tile = min(512, width)
    return call(
        "ffn_slope",
        ffn_slope_body,
        width // tile,
        [whole(p) for p in pieces] + [columns(a, tile) for a in (down, silu, slope)],
        [new_columns(tokens, width, tile)] * 2,
        [*pieces, down, silu, slope],
        2 * tokens * dim * width,
    )


def weight_grad(pieces, b, into=None):
    rows, dim = pieces[0].shape
    width = b.shape[1]
    tile = next(t for t in (512, 384, 256) if width % t == 0)
    step = min(512, dim)

    def body(*refs):
        left, b_ref, out = refs[:4], refs[4], refs[-1]
        for d in range(0, dim, step):
            total = None
            for i in range(4):
                term = dot(left[i][:, d : d + step], b_ref[i * rows : (i + 1) * rows], TN)
                total = term if total is None else total + term
            out[d : d + step] = total.astype(BF)

    return call(
        "weight_grad",
        body,
        width // tile,
        [whole(p) for p in pieces] + [columns(b, tile)] + ([] if into is None else [None]),
        [new_columns(dim, width if into is None else into.shape[1], tile)],
        [*pieces, b] + ([] if into is None else [into]),
        8 * rows * dim * width,
        aliases=None if into is None else {5: 0},
    )[0]


def back(acts, weights, pieces, tile):
    rows = acts[0].shape[0] // 4
    dim = weights[0][0].shape[0]
    tile = min(tile, dim)
    na, np_ = len(acts), len(pieces)

    def body(*refs):
        ws = refs[na * np_ : na * np_ + na]
        outs = refs[na * np_ + na :]
        for p in range(np_):
            total = None
            for a in range(na):
                term = dot(refs[p * na + a][...], ws[a][...], NT)
                total = term if total is None else total + term
            outs[p][...] = total.astype(BF)

    return call(
        "back",
        body,
        dim // tile,
        [((rows, a.shape[1]), lambda j, p=p: (p, 0), "held") for p in pieces for a in acts]
        + [
            ((tile, a.shape[1]), lambda j, c=c: (j, c)) for a, (_, c) in zip(acts, weights)
        ],
        [new_columns(rows, dim, tile)] * np_,
        [a for _ in pieces for a in acts] + [w for w, _ in weights],
        2 * np_ * rows * dim * sum(a.shape[1] for a in acts),
    )


def shifted(ref, place, near, seg, back_way):
    cur = ref[place * seg : (place + 1) * seg]
    row = jnp.maximum(near, 0) * seg + (0 if back_way else seg - 8)
    edge = ref[pl.ds(pl.multiple_of(row, 8), 8)]
    edge = jnp.where(near >= 0, edge, 0.0)
    return jnp.concatenate([cur, edge] if back_way else [edge, cur])


def conv_of(ref, place, near, seg, taps):
    ext = shifted(ref, place, near, seg, False)
    terms = [ext[6 : 6 + seg], ext[7 : 7 + seg], ext[8 : 8 + seg]]
    return taps[0] * terms[0] + taps[1] * terms[1] + taps[2] * terms[2], terms


def conv_body(places, *refs):
    pieces, (w, taps_ref, bgate, cgate, xgate, ygate, mixed) = refs[:4], refs[4:]
    rows = pieces[0].shape[0]
    tile = bgate.shape[1]
    for i in range(4):
        at = pl.ds(i * rows, rows)
        b = dot(pieces[i][...], w[:, :tile], NN)
        x = dot(pieces[i][...], w[:, 2 * tile :], NN)
        c = dot(pieces[i][...], w[:, tile : 2 * tile], NN)
        mixed[at] = b * x
        bgate[at] = b.astype(BF)
        cgate[at] = c.astype(BF)
        xgate[at] = x.astype(BF)
    taps = [taps_ref[k : k + 1] for k in range(3)]
    segs = places.shape[1]
    seg = mixed.shape[0] // segs
    for s in range(segs):
        conv, _ = conv_of(mixed, s, places[0, s], seg, taps)
        at = pl.ds(s * seg, seg)
        ygate[at] = (cgate[at].astype(F32) * conv).astype(BF)


def conv_forward(pieces, weights, taps, places, tile):
    chans = taps.shape[1]
    dim = weights.shape[0]
    tokens = 4 * pieces[0].shape[0]
    return call(
        "conv_fwd",
        conv_body,
        chans // tile,
        [whole(p) for p in pieces]
        + [((dim, 3 * tile), lambda j: (0, j)), ((3, tile), lambda j: (0, j))],
        [new_columns(tokens, chans, tile)] * 4,
        [*pieces, weights, taps],
        6 * tokens * dim * chans,
        [pltpu.VMEM((tokens, tile), F32)],
        [places],
    )


def conv_back_body(places, *refs):
    pieces = refs[:4]
    w, taps_ref, bgate, cgate, xgate, ygate, dproj, tap_grad, out_grad, mixed, dconv = refs[4:]
    taps = [taps_ref[k : k + 1] for k in range(3)]
    segs = places.shape[1]
    tokens, tile = mixed.shape
    seg = tokens // segs
    mixed[...] = bgate[...].astype(F32) * xgate[...].astype(F32)
    rows = pieces[0].shape[0]
    sums = [jnp.zeros((1, tile), F32) for _ in range(3)]
    for i in range(4):
        dy = dot(pieces[i][...], w[...], NN)
        for s in range(i * segs // 4, (i + 1) * segs // 4):
            at = pl.ds(s * seg, seg)
            low = s * seg - i * rows
            dys = dy[low : low + seg]
            conv, terms = conv_of(mixed, s, places[0, s], seg, taps)
            dc = dys * cgate[at].astype(F32)
            dconv[at] = dc
            dproj[at, tile : 2 * tile] = (dys * conv).astype(BF)
            sums = [v + jnp.sum(dc * term, axis=0, keepdims=True) for v, term in zip(sums, terms)]
    for k in range(3):
        tap_grad[k : k + 1] = sums[k]
    for s in range(segs):
        at = pl.ds(s * seg, seg)
        ext = shifted(dconv, s, places[1, s], seg, True)
        dbx = taps[2] * ext[:seg] + taps[1] * ext[1 : 1 + seg] + taps[0] * ext[2 : 2 + seg]
        dproj[at, :tile] = (dbx * xgate[at].astype(F32)).astype(BF)
        dproj[at, 2 * tile :] = (dbx * bgate[at].astype(F32)).astype(BF)
    dim = pieces[0].shape[1]
    for d in range(0, dim, 512):
        total = None
        for i in range(4):
            term = dot(pieces[i][:, d : d + 512], ygate[i * rows : (i + 1) * rows], TN)
            total = term if total is None else total + term
        out_grad[d : d + 512] = total.astype(BF)


def conv_backward(pieces, weights, taps, saved, places, tile):
    chans = taps.shape[1]
    dim = weights.shape[0]
    tokens = 4 * pieces[0].shape[0]
    return call(
        "conv_bwd",
        conv_back_body,
        chans // tile,
        [whole(p) for p in pieces]
        + [columns(weights, tile, 3 * chans // tile), ((3, tile), lambda j: (0, j))]
        + [columns(a, tile) for a in saved],
        [
            ((tokens, 3 * tile), lambda j: (0, j), (tokens, 3 * chans), BF),
            ((3, tile), lambda j: (0, j), (3, chans), F32),
            ((dim, tile), lambda j: (0, 3 * chans // tile + j), (dim, 4 * chans), BF),
        ],
        [*pieces, weights, taps, *saved],
        4 * tokens * dim * chans,
        [pltpu.VMEM((tokens, tile), F32)] * 2,
        [places],
    )


def local(
    sizes,
    tokens,
    in_weight,
    conv_taps,
    out_weight,
    gate_weight,
    up_weight,
    down_weight,
    norm_gain1,
    norm_gain2,
    out_grad,
):
    ndp, nt = sizes
    square = Square(nt)
    chans, dim = out_weight.shape[0], tokens.shape[2]
    offset = square.t * chans
    tile = min(256, chans)
    places = square.places()
    taps = lax.dynamic_slice_in_dim(conv_taps, offset, chans, 1)
    dp_gather = lambda v: lax.all_gather(v, "dp", axis=0, tiled=True)
    dp_scatter = lambda v: lax.psum_scatter(v, "dp", scatter_dimension=0, tiled=True)

    conv_shard = jnp.concatenate(
        [in_weight[k, :, c : c + tile] for c in range(0, chans, tile) for k in range(3)]
        + [out_weight.T],
        axis=1,
    )
    conv_w = dp_gather(conv_shard)
    down_shard = down_weight.T

    hidden = tokens[0].astype(F32)
    scale1 = rms_scale(hidden)
    n1, _ = square.gather((hidden * scale1 * norm_gain1).astype(BF))
    cot = out_grad[0]
    gate_w = dp_gather(after(gate_weight, conv_w, n1[1], n1[3]))
    g_gather = square.gather_steps(after(cot, n1[1], n1[3]))
    g_first = next(g_gather)
    saved = conv_forward(n1, conv_w, taps, places, tile)
    ygate = saved[3]
    far = back([after(ygate, *g_first)], [(conv_w, 3)], (1, 3), 1024)
    near = back([after(ygate, far[0])], [(conv_w, 3)], (0, 2), 1024)
    branch, mid = square.finish(near, square.begin(far))
    up_w = dp_gather(after(up_weight, gate_w, *mid))
    second = hidden + branch
    scale2 = rms_scale(second)
    n2, n2_first = square.gather((second * scale2 * norm_gain2).astype(BF))
    down_w = dp_gather(after(down_shard, up_w, n2[1], n2[3]))
    g = g_gather.send((n2[1], n2[3]))

    act, silu, slope = ffn_gate(n2, gate_w, up_w)
    down_part = weight_grad(first_after(g, act), act)
    down_owned = dp_scatter(down_part)
    dgate, dup = ffn_slope(first_after(g, down_part), down_w, silu, slope)
    pair = [(gate_w, 0), (up_w, 0)]
    gate_part = weight_grad(first_after(n2, dgate), dgate)
    far = back([after(dgate, gate_part), dup], pair, (1, 3), 512)
    near = back([after(dgate, far[0]), dup], pair, (0, 2), 512)
    ffn = back([after(act, near[0])], [(down_w, 0)], (1, 3, 0, 2), 512)
    dnormed2, mid = square.finish(near, square.begin(far), ffn[0])
    gate_owned = dp_scatter(after(gate_part, down_owned, *mid))
    up_part = weight_grad(first_after(n2, *mid), dup)
    dsecond_norm, gain2_part = norm_back(second, scale2, norm_gain2, dnormed2)
    dsecond = cot.astype(F32) + dsecond_norm
    dbr, dbr_first = square.gather(dsecond.astype(BF))
    up_owned = dp_scatter(after(up_part, gate_owned, dbr[1], dbr[3]))

    dproj, tap_part, conv_part = conv_backward(dbr, conv_w, taps, saved, places, tile)
    far = back([dproj], [(conv_w, 0)], (1, 3), 512)
    near = back([after(dproj, far[0])], [(conv_w, 0)], (0, 2), 512)
    conv_part = weight_grad(first_after(n1, near[0]), dproj, conv_part)
    dnormed, mid = square.finish(near, square.begin(far))
    ffn, _ = square.finish(ffn[2:], square.begin([after(v, *mid) for v in ffn[:2]]))
    conv_owned = dp_scatter(after(conv_part, up_owned, *mid))
    block_out = (second + ffn).astype(BF)
    dhidden_norm, gain1_part = norm_back(hidden, scale1, norm_gain1, dnormed)
    tokens_grad = dsecond + dhidden_norm

    wide = lax.dynamic_update_slice_in_dim(
        jnp.zeros((3, conv_taps.shape[1]), F32), tap_part, offset, 1
    )
    small = jnp.concatenate(
        [gain1_part[None], gain2_part[None], wide, jnp.zeros_like(wide)]
    )
    small = total_of(small, (("tensor", nt), ("dp", ndp)))
    in_owned = conv_owned[:, : 3 * chans].reshape(-1, chans // tile, 3, tile)
    in_owned = in_owned.transpose(2, 0, 1, 3)
    return (
        block_out[None],
        tokens_grad[None],
        in_owned.reshape(3, -1, chans).astype(F32),
        small[2:5],
        conv_owned[:, 3 * chans :].T.astype(F32),
        gate_owned.astype(F32),
        up_owned.astype(F32),
        down_owned.T.astype(F32),
        small[0],
        small[1],
    )


def solution(mesh):
    in_specs = (
        P("dp", "tensor", None),
        P(None, "dp", "tensor"),
        P(),
        P("tensor", "dp"),
        P("dp", "tensor"),
        P("dp", "tensor"),
        P("tensor", "dp"),
        P(),
        P(),
        P("dp", "tensor", None),
    )
    out_specs = (
        P("dp", "tensor", None),
        P("dp", "tensor", None),
        P(None, "dp", "tensor"),
        P(),
        P("tensor", "dp"),
        P("dp", "tensor"),
        P("dp", "tensor"),
        P("tensor", "dp"),
        P(),
        P(),
    )
    sizes = (mesh.shape["dp"], mesh.shape["tensor"])
    return jax.shard_map(
        functools.partial(local, sizes),
        mesh=mesh,
        in_specs=in_specs,
        out_specs=out_specs,
        check_vma=False,
    )
```

```python
import functools
import math

import jax
import jax.numpy as jnp
import numpy as np
from jax import lax
from jax.experimental import pallas as pl
from jax.experimental.pallas import tpu as pltpu
from jax.sharding import PartitionSpec as P

EPS = 1e-05
BF = jnp.bfloat16
F32 = jnp.float32
VMEM_LIMIT = 58 * 2**20
COST = 0.2
NN = (((1,), (0,)), ((), ()))
NT = (((1,), (1,)), ((), ()))
TN = (((0,), (0,)), ((), ()))


def dot(a, b, dims):
    return lax.dot_general(a, b, dims, preferred_element_type=F32)


def after(value, *others):
    if not others:
        return value
    return lax.optimization_barrier((value, others))[0]


def first_after(pieces, *others):
    return [after(pieces[0], *others)] + list(pieces[1:])


def rms_scale(values):
    return lax.rsqrt(jnp.mean(values * values, axis=-1, keepdims=True) + EPS)


def norm_back(hidden, scale, gain, grad):
    scaled = gain * grad
    back = scale * scaled - hidden * scale**3 * jnp.mean(scaled * hidden, axis=-1, keepdims=True)
    return back, jnp.sum(grad * hidden * scale, axis=0)


class Square:
    def __init__(self, nt):
        self.nt = nt
        self.t = lax.axis_index("tensor")
        bits = [1 << i for i in range(int(math.log2(nt)))]
        self.orders = (bits, bits[::-1])
        self.lists = []
        for order in self.orders:
            seen = [0]
            for bit in order:
                seen = seen + [r ^ bit for r in seen]
            self.lists.append(seen)

    def flip(self, value, bit):
        return lax.ppermute(value, "tensor", [(t, t ^ bit) for t in range(self.nt)])

    def gather(self, rows, *gates):
        half = rows.shape[0] // 2
        curs = [rows[:half], rows[half:]]
        depth = len(self.orders[0])
        first = None
        for level in range(depth):
            came = [self.flip(c, o[level]) for c, o in zip(curs, self.orders)]
            first = first or came
            if level < depth - 1:
                curs = [after(jnp.concatenate([c, r]), *gates) for c, r in zip(curs, came)]
        return [curs[0], came[0], curs[1], came[1]], first

    def gather_steps(self, rows):
        half = rows.shape[0] // 2
        curs = [rows[:half], rows[half:]]
        depth = len(self.orders[0])
        came = None
        for level in range(depth):
            gates = yield curs, came
            curs = [after(c, *gates) for c in curs]
            came = [self.flip(c, o[level]) for c, o in zip(curs, self.orders)]
            if level < depth - 1:
                curs = [jnp.concatenate([c, r]) for c, r in zip(curs, came)]
        yield [curs[0], came[0], curs[1], came[1]], None

    def begin(self, far):
        return [self.flip(s, o[-1]) for s, o in zip(far, self.orders)]

    def finish(self, near, came, *gates):
        depth = len(self.orders[0])
        total = lambda terms: sum(v.astype(F32) for v in terms)
        parts = [[k, r] for k, r in zip(near, came)]
        sends = came
        for level in range(depth - 1, 0, -1):
            half = parts[0][0].shape[0] // 2
            sends = [after(total([v[half:] for v in p]).astype(BF), *gates) for p in parts]
            came = [self.flip(s, o[level - 1]) for s, o in zip(sends, self.orders)]
            parts = [[v[:half] for v in p] + [r] for p, r in zip(parts, came)]
        return jnp.concatenate([total(p) for p in parts]), sends, came

    def places(self):
        index = {}
        for h, seen in enumerate(self.lists):
            for i, r in enumerate(seen):
                index[r, h] = h * self.nt + i
        table = np.zeros((self.nt, 2, 2 * self.nt), np.int32)
        for t in range(self.nt):
            for (r, h), i in index.items():
                at = t ^ r
                if h:
                    table[t, 0, i] = index[r, 0]
                    table[t, 1, i] = -1 if at == self.nt - 1 else index[(at + 1) ^ t, 0]
                else:
                    table[t, 0, i] = -1 if at == 0 else index[(at - 1) ^ t, 1]
                    table[t, 1, i] = index[r, 1]
        return lax.dynamic_index_in_dim(jnp.asarray(table), self.t, keepdims=False)


def total_of(value, axis, size):
    bit = 1
    while bit < size:
        value = value + lax.ppermute(value, axis, [(i, i ^ bit) for i in range(size)])
        bit *= 2
    return value


def call(name, body, grid, ins, outs, args, flops, scratch=(), scalars=(), aliases=None):
    held = lambda spec: pl.BlockSpec(memory_space=pl.ANY) if spec is None else pl.BlockSpec(
        spec[0],
        lambda j, *_: spec[1](j),
        **({"pipeline_mode": pl.Buffered(1)} if len(spec) > 2 and spec[2] == "held" else {}),
    )
    moved = sum(math.prod(a.shape) * a.dtype.itemsize for a in args)
    moved += sum(math.prod(o[2]) * jnp.dtype(o[3]).itemsize for o in outs)
    return pl.pallas_call(
        body,
        grid_spec=pltpu.PrefetchScalarGridSpec(
            num_scalar_prefetch=len(scalars),
            grid=(grid,),
            in_specs=[held(s) for s in ins],
            out_specs=[pl.BlockSpec(o[0], lambda j, *_, o=o: o[1](j)) for o in outs],
            scratch_shapes=list(scratch),
        ),
        out_shape=[jax.ShapeDtypeStruct(o[2], o[3]) for o in outs],
        name=name,
        input_output_aliases=aliases or {},
        compiler_params=pltpu.CompilerParams(vmem_limit_bytes=VMEM_LIMIT),
        cost_estimate=pl.CostEstimate(
            flops=int(flops * COST), bytes_accessed=int(moved * COST), transcendentals=0
        ),
    )(*scalars, *args)


def whole(a):
    return (a.shape, lambda j: (0,) * a.ndim, "held")


def columns(a, tile, start=0):
    return ((a.shape[0], tile), lambda j: (0, start + j))


def new_columns(rows, width, tile, dtype=BF):
    return ((rows, tile), lambda j: (0, j), (rows, width), dtype)


def pack(in_weight, out_weight, tile):
    kinds, depth, chans = in_weight.shape

    def body(win, wout, packed):
        for j in range(chans // tile):
            for k in range(kinds):
                at = (j * kinds + k) * tile
                packed[:, at : at + tile] = win[k, :, j * tile : (j + 1) * tile]
        packed[:, kinds * chans :] = wout[...].astype(F32).T.astype(BF)

    width = (kinds + 1) * chans
    return call(
        "pack",
        body,
        1,
        [whole(in_weight), whole(out_weight)],
        [new_columns(depth, width, width)],
        [in_weight, out_weight],
        0,
    )[0]


def gate_body(*refs):
    pieces, (gw, uw, act, silu, slope) = refs[:4], refs[4:]
    rows = pieces[0].shape[0]
    for i in range(4):
        at = pl.ds(i * rows, rows)
        gate = dot(pieces[i][...], gw[...], NN)
        up = dot(pieces[i][...], uw[...], NN)
        sig = jax.nn.sigmoid(gate)
        s = gate * sig
        act[at] = (s * up).astype(BF)
        silu[at] = s.astype(BF)
        slope[at] = (up * sig * (1.0 + gate * (1.0 - sig))).astype(BF)


def ffn_gate(pieces, gate, up):
    dim, width = gate.shape
    tokens = 4 * pieces[0].shape[0]
    tile = min(256, width)
    return call(
        "ffn_gate",
        gate_body,
        width // tile,
        [whole(p) for p in pieces] + [columns(gate, tile), columns(up, tile)],
        [new_columns(tokens, width, tile)] * 3,
        [*pieces, gate, up],
        4 * tokens * dim * width,
    )


def ffn_slope_body(*refs):
    pieces, (w, silu, slope, dgate, dup) = refs[:4], refs[4:]
    rows = pieces[0].shape[0]
    for i in range(4):
        at = pl.ds(i * rows, rows)
        dact = dot(pieces[i][...], w[...], NN)
        dgate[at] = (dact * slope[at].astype(F32)).astype(BF)
        dup[at] = (dact * silu[at].astype(F32)).astype(BF)


def ffn_slope(pieces, down, silu, slope):
    dim, width = down.shape
    tokens = 4 * pieces[0].shape[0]
    tile = min(512, width)
    return call(
        "ffn_slope",
        ffn_slope_body,
        width // tile,
        [whole(p) for p in pieces] + [columns(a, tile) for a in (down, silu, slope)],
        [new_columns(tokens, width, tile)] * 2,
        [*pieces, down, silu, slope],
        2 * tokens * dim * width,
    )


def transposed_dot(left, b, columns):
    rows = left[0].shape[0]
    total = None
    for i in range(4):
        term = dot(left[i][:, columns], b[i * rows : (i + 1) * rows], TN)
        total = term if total is None else total + term
    return total.astype(BF)


def weight_grad(pieces, b, into=None):
    rows, dim = pieces[0].shape
    width = b.shape[1]
    tile = next(t for t in (512, 384, 256) if width % t == 0)
    step = min(512, dim)
    into = [] if into is None else [into]

    def body(*refs):
        for d in range(0, dim, step):
            refs[-1][d : d + step] = transposed_dot(refs[:4], refs[4], slice(d, d + step))

    return call(
        "weight_grad",
        body,
        width // tile,
        [whole(p) for p in pieces] + [columns(b, tile)] + [None] * len(into),
        [new_columns(dim, into[0].shape[1] if into else width, tile)],
        [*pieces, b, *into],
        8 * rows * dim * width,
        aliases={5: 0} if into else None,
    )[0]


def back(acts, weights, pieces, tile, sums=None):
    rows = acts[0].shape[0] // 4
    dim = weights[0][0].shape[0]
    tile = min(tile, dim)
    na, np_ = len(acts), len(pieces)
    extra = [] if sums is None else [sums[p] for p in pieces]

    def body(*refs):
        ws = refs[na * np_ : na * np_ + na]
        outs = refs[na * np_ + na + len(extra) :]
        summed = None
        for p in range(np_):
            total = None
            for a in range(na):
                term = dot(refs[p * na + a][...], ws[a][...], NT)
                total = term if total is None else total + term
            outs[p][...] = total.astype(BF)
            if extra:
                term = total * refs[na * np_ + na + p][...].astype(F32)
                term = jnp.sum(term, axis=0, keepdims=True)
                summed = term if summed is None else summed + term
        if extra:
            outs[np_][...] = summed

    return call(
        "back",
        body,
        dim // tile,
        [((rows, a.shape[1]), lambda j, p=p: (p, 0), "held") for p in pieces for a in acts]
        + [((tile, a.shape[1]), lambda j, c=c: (j, c)) for a, (_, c) in zip(acts, weights)]
        + [columns(v, tile) for v in extra],
        [new_columns(rows, dim, tile)] * np_
        + ([new_columns(1, dim, tile, F32)] if extra else []),
        [a for _ in pieces for a in acts] + [w for w, _ in weights] + extra,
        2 * np_ * rows * dim * sum(a.shape[1] for a in acts),
    )


def shifted(ref, place, near, seg, back_way):
    cur = ref[place * seg : (place + 1) * seg]
    row = jnp.maximum(near, 0) * seg + (0 if back_way else seg - 8)
    edge = ref[pl.ds(pl.multiple_of(row, 8), 8)]
    edge = jnp.where(near >= 0, edge, 0.0)
    return jnp.concatenate([cur, edge] if back_way else [edge, cur])


def conv_of(ref, place, near, seg, taps):
    ext = shifted(ref, place, near, seg, False)
    terms = [ext[6 : 6 + seg], ext[7 : 7 + seg], ext[8 : 8 + seg]]
    return taps[0] * terms[0] + taps[1] * terms[1] + taps[2] * terms[2], terms


def conv_body(places, *refs):
    pieces, (w, taps_ref, bgate, cgate, xgate, ygate, mixed) = refs[:4], refs[4:]
    rows = pieces[0].shape[0]
    tile = bgate.shape[1]
    for i in range(4):
        at = pl.ds(i * rows, rows)
        b = dot(pieces[i][...], w[:, :tile], NN)
        x = dot(pieces[i][...], w[:, 2 * tile :], NN)
        c = dot(pieces[i][...], w[:, tile : 2 * tile], NN)
        mixed[at] = b * x
        bgate[at] = b.astype(BF)
        cgate[at] = c.astype(BF)
        xgate[at] = x.astype(BF)
    taps = [taps_ref[k : k + 1] for k in range(3)]
    segs = places.shape[1]
    seg = mixed.shape[0] // segs
    for s in range(segs):
        conv, _ = conv_of(mixed, s, places[0, s], seg, taps)
        at = pl.ds(s * seg, seg)
        ygate[at] = (cgate[at].astype(F32) * conv).astype(BF)


def conv_forward(pieces, weights, taps, places, tile):
    chans = taps.shape[1]
    dim = weights.shape[0]
    tokens = 4 * pieces[0].shape[0]
    return call(
        "conv_fwd",
        conv_body,
        chans // tile,
        [whole(p) for p in pieces]
        + [((dim, 3 * tile), lambda j: (0, j)), ((3, tile), lambda j: (0, j))],
        [new_columns(tokens, chans, tile)] * 4,
        [*pieces, weights, taps],
        6 * tokens * dim * chans,
        [pltpu.VMEM((tokens, tile), F32)],
        [places],
    )


def conv_back_body(places, *refs):
    pieces = refs[:4]
    w, taps_ref, bgate, cgate, xgate, ygate, dproj, tap_grad, out_grad, mixed, dconv = refs[4:]
    taps = [taps_ref[k : k + 1] for k in range(3)]
    segs = places.shape[1]
    tokens, tile = mixed.shape
    seg = tokens // segs
    mixed[...] = bgate[...].astype(F32) * xgate[...].astype(F32)
    rows = pieces[0].shape[0]
    sums = [jnp.zeros((1, tile), F32) for _ in range(3)]
    for i in range(4):
        dy = dot(pieces[i][...], w[...], NN)
        for s in range(i * segs // 4, (i + 1) * segs // 4):
            at = pl.ds(s * seg, seg)
            low = s * seg - i * rows
            dys = dy[low : low + seg]
            conv, terms = conv_of(mixed, s, places[0, s], seg, taps)
            dc = dys * cgate[at].astype(F32)
            dconv[at] = dc
            dproj[at, tile : 2 * tile] = (dys * conv).astype(BF)
            sums = [v + jnp.sum(dc * term, axis=0, keepdims=True) for v, term in zip(sums, terms)]
    for k in range(3):
        tap_grad[k : k + 1] = sums[k]
    for s in range(segs):
        at = pl.ds(s * seg, seg)
        ext = shifted(dconv, s, places[1, s], seg, True)
        dbx = taps[2] * ext[:seg] + taps[1] * ext[1 : 1 + seg] + taps[0] * ext[2 : 2 + seg]
        dproj[at, :tile] = (dbx * xgate[at].astype(F32)).astype(BF)
        dproj[at, 2 * tile :] = (dbx * bgate[at].astype(F32)).astype(BF)
    dim = pieces[0].shape[1]
    for d in range(0, dim, 512):
        out_grad[d : d + 512] = transposed_dot(pieces, ygate, slice(d, d + 512))


def conv_backward(pieces, weights, taps, saved, places, tile):
    chans = taps.shape[1]
    dim = weights.shape[0]
    tokens = 4 * pieces[0].shape[0]
    return call(
        "conv_bwd",
        conv_back_body,
        chans // tile,
        [whole(p) for p in pieces]
        + [columns(weights, tile, 3 * chans // tile), ((3, tile), lambda j: (0, j))]
        + [columns(a, tile) for a in saved],
        [
            ((tokens, 3 * tile), lambda j: (0, j), (tokens, 3 * chans), BF),
            ((3, tile), lambda j: (0, j), (3, chans), F32),
            ((dim, tile), lambda j: (0, 3 * chans // tile + j), (dim, 4 * chans), BF),
        ],
        [*pieces, weights, taps, *saved],
        4 * tokens * dim * chans,
        [pltpu.VMEM((tokens, tile), F32)] * 2,
        [places],
    )


def local(
    sizes,
    tokens,
    in_weight,
    conv_taps,
    out_weight,
    gate_weight,
    up_weight,
    down_weight,
    norm_gain1,
    norm_gain2,
    out_grad,
):
    ndp, nt = sizes
    square = Square(nt)
    chans, dim = out_weight.shape[0], tokens.shape[2]
    offset = square.t * chans
    tile = min(256, chans)
    places = square.places()
    taps = lax.dynamic_slice_in_dim(conv_taps, offset, chans, 1)
    dp_gather = lambda v: lax.all_gather(v, "dp", axis=0, tiled=True)
    dp_scatter = lambda v: lax.psum_scatter(v, "dp", scatter_dimension=0, tiled=True)

    conv_shard = pack(in_weight, out_weight, tile)
    conv_w = dp_gather(conv_shard)
    down_shard = down_weight.T

    hidden = tokens[0].astype(F32)
    scale1 = rms_scale(hidden)
    cot = out_grad[0]
    g_gather = square.gather_steps(cot)
    g_one, _ = next(g_gather)
    n1, _ = square.gather((hidden * scale1 * norm_gain1).astype(BF), *g_one)
    gate_w = dp_gather(after(gate_weight, conv_w, n1[1], n1[3]))
    g_two, g_first = g_gather.send((n1[1], n1[3]))
    saved = conv_forward(n1, conv_w, taps, places, tile)
    ygate = saved[3]
    far = back([after(ygate, *g_first)], [(conv_w, 3)], (1, 3), 1024)
    near = back([after(ygate, far[0])], [(conv_w, 3)], (0, 2), 1024)
    branch, mid, _ = square.finish(near, square.begin(far), *g_two)
    up_w = dp_gather(after(up_weight, gate_w, *mid))
    second = hidden + branch
    scale2 = rms_scale(second)
    n2, n2_first = square.gather((second * scale2 * norm_gain2).astype(BF))
    down_w = dp_gather(after(down_shard, up_w, n2[1], n2[3]))
    while g_first:
        g_two, g_first = g_gather.send((n2[1], n2[3]))
    g = g_two

    act, silu, slope = ffn_gate(n2, gate_w, up_w)
    down_part = weight_grad(first_after(g, act), act)
    down_owned = dp_scatter(down_part)
    dgate, dup = ffn_slope(first_after(g, down_part), down_w, silu, slope)
    pair = [(gate_w, 0), (up_w, 0)]
    far = back([dgate, dup], pair, (1, 3), 512)
    near = back([after(dgate, far[0]), dup], pair, (0, 2), 512)
    gate_part = weight_grad(first_after(n2, near[0]), dgate)
    dnormed2, mid, _ = square.finish(near, square.begin(far), gate_part)
    gate_owned = dp_scatter(after(gate_part, down_owned, *mid))
    ffn = back([after(act, *mid)], [(down_w, 0)], (1, 3, 0, 2), 512)
    dsecond_norm, gain2_part = norm_back(second, scale2, norm_gain2, dnormed2)
    dsecond = cot.astype(F32) + dsecond_norm
    sent = after(dsecond.astype(BF), ffn[0])
    dbr, dbr_first = square.gather(sent)
    up_part = weight_grad(first_after(n2, sent), dup)
    up_owned = dp_scatter(after(up_part, gate_owned, dbr[1], dbr[3]))

    dproj, tap_part, conv_part = conv_backward(
        first_after(dbr, up_part), conv_w, taps, saved, places, tile
    )
    came = square.begin([after(v, dbr[1], dbr[3]) for v in ffn[:2]])
    far = back([dproj], [(conv_w, 0)], (1, 3), 512, n1)
    conv_part = weight_grad(first_after(n1, far[0], *came), dproj, conv_part)
    ffn, ffn_sends, _ = square.finish(ffn[2:], came)
    near = back([after(dproj, conv_part, *ffn_sends)], [(conv_w, 0)], (0, 2), 512, n1)
    first_came = square.begin(far[:2])
    dnormed, mid, last_came = square.finish(near[:2], first_came)
    conv_owned = dp_scatter(after(conv_part, up_owned, *first_came))
    gain1_part = (far[2] + near[2])[0] / norm_gain1
    block_out = (second + ffn).astype(BF)
    dhidden_norm, _ = norm_back(hidden, scale1, norm_gain1, dnormed)
    tokens_grad = dsecond + dhidden_norm

    wide = lax.dynamic_update_slice_in_dim(
        jnp.zeros((3, conv_taps.shape[1]), F32), tap_part, offset, 1
    )
    small = jnp.concatenate(
        [gain1_part[None], gain2_part[None], wide, jnp.zeros_like(wide)]
    )
    small = total_of(after(small, *first_came), "dp", ndp)
    small = total_of(after(small, *last_came), "tensor", nt)
    in_owned = conv_owned[:, : 3 * chans].reshape(-1, chans // tile, 3, tile)
    in_owned = in_owned.transpose(2, 0, 1, 3)
    return (
        block_out[None],
        tokens_grad[None],
        in_owned.reshape(3, -1, chans).astype(F32),
        small[2:5],
        conv_owned[:, 3 * chans :].T.astype(F32),
        gate_owned.astype(F32),
        up_owned.astype(F32),
        down_owned.T.astype(F32),
        small[0],
        small[1],
    )


def solution(mesh):
    in_specs = (
        P("dp", "tensor", None),
        P(None, "dp", "tensor"),
        P(),
        P("tensor", "dp"),
        P("dp", "tensor"),
        P("dp", "tensor"),
        P("tensor", "dp"),
        P(),
        P(),
        P("dp", "tensor", None),
    )
    out_specs = (
        P("dp", "tensor", None),
        P("dp", "tensor", None),
        P(None, "dp", "tensor"),
        P(),
        P("tensor", "dp"),
        P("dp", "tensor"),
        P("dp", "tensor"),
        P("tensor", "dp"),
        P(),
        P(),
    )
    sizes = (mesh.shape["dp"], mesh.shape["tensor"])
    return jax.shard_map(
        functools.partial(local, sizes),
        mesh=mesh,
        in_specs=in_specs,
        out_specs=out_specs,
        check_vma=False,
    )
```

```python
import functools
import math

import jax
import jax.numpy as jnp
import numpy as np
from jax import lax
from jax.experimental import pallas as pl
from jax.experimental.pallas import tpu as pltpu
from jax.sharding import PartitionSpec as P

EPS = 1e-05
BF = jnp.bfloat16
F32 = jnp.float32
VMEM_LIMIT = 58 * 2**20
COST = 0.2
NN = (((1,), (0,)), ((), ()))
NT = (((1,), (1,)), ((), ()))
TN = (((0,), (0,)), ((), ()))


def dot(a, b, dims):
    return lax.dot_general(a, b, dims, preferred_element_type=F32)


def after(value, *others):
    if not others:
        return value
    return lax.optimization_barrier((value, others))[0]


def first_after(pieces, *others):
    return [after(pieces[0], *others)] + list(pieces[1:])


def rms_scale(values):
    return lax.rsqrt(jnp.mean(values * values, axis=-1, keepdims=True) + EPS)


def norm_back(hidden, scale, gain, grad):
    scaled = gain * grad
    back = scale * scaled - hidden * scale**3 * jnp.mean(scaled * hidden, axis=-1, keepdims=True)
    return back, jnp.sum(grad * hidden * scale, axis=0)


class Square:
    def __init__(self, nt):
        self.nt = nt
        self.t = lax.axis_index("tensor")
        bits = [1 << i for i in range(int(math.log2(nt)))]
        self.orders = (bits, bits[::-1])
        self.lists = []
        for order in self.orders:
            seen = [0]
            for bit in order:
                seen = seen + [r ^ bit for r in seen]
            self.lists.append(seen)

    def flip(self, value, bit):
        return lax.ppermute(value, "tensor", [(t, t ^ bit) for t in range(self.nt)])

    def gather(self, rows, *gates):
        half = rows.shape[0] // 2
        curs = [rows[:half], rows[half:]]
        depth = len(self.orders[0])
        first = None
        for level in range(depth):
            came = [self.flip(c, o[level]) for c, o in zip(curs, self.orders)]
            first = first or came
            if level < depth - 1:
                curs = [after(jnp.concatenate([c, r]), *gates) for c, r in zip(curs, came)]
        return [curs[0], came[0], curs[1], came[1]], first

    def gather_steps(self, rows):
        half = rows.shape[0] // 2
        curs = [rows[:half], rows[half:]]
        depth = len(self.orders[0])
        came = None
        for level in range(depth):
            gates = yield curs, came
            curs = [after(c, *gates) for c in curs]
            came = [self.flip(c, o[level]) for c, o in zip(curs, self.orders)]
            if level < depth - 1:
                curs = [jnp.concatenate([c, r]) for c, r in zip(curs, came)]
        yield [curs[0], came[0], curs[1], came[1]], None

    def begin(self, far):
        return [self.flip(s, o[-1]) for s, o in zip(far, self.orders)]

    def finish(self, near, came, *gates):
        depth = len(self.orders[0])
        total = lambda terms: sum(v.astype(F32) for v in terms)
        parts = [[k, r] for k, r in zip(near, came)]
        sends = came
        for level in range(depth - 1, 0, -1):
            half = parts[0][0].shape[0] // 2
            sends = [after(total([v[half:] for v in p]).astype(BF), *gates) for p in parts]
            came = [self.flip(s, o[level - 1]) for s, o in zip(sends, self.orders)]
            parts = [[v[:half] for v in p] + [r] for p, r in zip(parts, came)]
        return jnp.concatenate([total(p) for p in parts]), sends, came

    def places(self):
        index = {}
        for h, seen in enumerate(self.lists):
            for i, r in enumerate(seen):
                index[r, h] = h * self.nt + i
        table = np.zeros((self.nt, 2, 2 * self.nt), np.int32)
        for t in range(self.nt):
            for (r, h), i in index.items():
                at = t ^ r
                if h:
                    table[t, 0, i] = index[r, 0]
                    table[t, 1, i] = -1 if at == self.nt - 1 else index[(at + 1) ^ t, 0]
                else:
                    table[t, 0, i] = -1 if at == 0 else index[(at - 1) ^ t, 1]
                    table[t, 1, i] = index[r, 1]
        return lax.dynamic_index_in_dim(jnp.asarray(table), self.t, keepdims=False)


def total_of(value, axis, size):
    bit = 1
    while bit < size:
        value = value + lax.ppermute(value, axis, [(i, i ^ bit) for i in range(size)])
        bit *= 2
    return value


def call(name, body, grid, ins, outs, args, flops, scratch=(), scalars=(), aliases=None, weight=1.0):
    held = lambda spec: pl.BlockSpec(memory_space=pl.ANY) if spec is None else pl.BlockSpec(
        spec[0],
        lambda j, *_: spec[1](j),
        **({"pipeline_mode": pl.Buffered(1)} if len(spec) > 2 and spec[2] == "held" else {}),
    )
    moved = sum(math.prod(a.shape) * a.dtype.itemsize for a in args)
    moved += sum(math.prod(o[2]) * jnp.dtype(o[3]).itemsize for o in outs)
    return pl.pallas_call(
        body,
        grid_spec=pltpu.PrefetchScalarGridSpec(
            num_scalar_prefetch=len(scalars),
            grid=(grid,),
            in_specs=[held(s) for s in ins],
            out_specs=[pl.BlockSpec(o[0], lambda j, *_, o=o: o[1](j)) for o in outs],
            scratch_shapes=list(scratch),
        ),
        out_shape=[jax.ShapeDtypeStruct(o[2], o[3]) for o in outs],
        name=name,
        input_output_aliases=aliases or {},
        compiler_params=pltpu.CompilerParams(vmem_limit_bytes=VMEM_LIMIT),
        cost_estimate=pl.CostEstimate(
            flops=int(flops * COST * weight),
            bytes_accessed=int(moved * COST * weight),
            transcendentals=0,
        ),
    )(*scalars, *args)


def whole(a):
    return (a.shape, lambda j: (0,) * a.ndim, "held")


def columns(a, tile, start=0):
    return ((a.shape[0], tile), lambda j: (0, start + j))


def new_columns(rows, width, tile, dtype=BF):
    return ((rows, tile), lambda j: (0, j), (rows, width), dtype)


def pack(in_weight, out_weight, tile):
    kinds, depth, chans = in_weight.shape

    def body(win, wout, packed):
        for j in range(chans // tile):
            for k in range(kinds):
                at = (j * kinds + k) * tile
                packed[:, at : at + tile] = win[k, :, j * tile : (j + 1) * tile]
        packed[:, kinds * chans :] = wout[...].astype(F32).T.astype(BF)

    width = (kinds + 1) * chans
    return call(
        "pack",
        body,
        1,
        [whole(in_weight), whole(out_weight)],
        [new_columns(depth, width, width)],
        [in_weight, out_weight],
        0,
    )[0]


def unpack(packed, chans, tile):
    depth = packed.shape[0]
    kinds = packed.shape[1] // chans - 1

    def body(src, win, wout):
        for j in range(chans // tile):
            for k in range(kinds):
                at = (j * kinds + k) * tile
                win[k, :, j * tile : (j + 1) * tile] = src[:, at : at + tile].astype(F32)
        wout[...] = src[:, kinds * chans :].astype(F32).T

    return call(
        "unpack",
        body,
        1,
        [whole(packed)],
        [
            ((kinds, depth, chans), lambda j: (0, 0, 0), (kinds, depth, chans), F32),
            ((chans, depth), lambda j: (0, 0), (chans, depth), F32),
        ],
        [packed],
        0,
    )


def gate_body(*refs):
    pieces, (gw, uw, act, silu, slope) = refs[:4], refs[4:]
    rows = pieces[0].shape[0]
    for i in range(4):
        at = pl.ds(i * rows, rows)
        gate = dot(pieces[i][...], gw[...], NN)
        up = dot(pieces[i][...], uw[...], NN)
        sig = jax.nn.sigmoid(gate)
        s = gate * sig
        act[at] = (s * up).astype(BF)
        silu[at] = s.astype(BF)
        slope[at] = (up * sig * (1.0 + gate * (1.0 - sig))).astype(BF)


def ffn_gate(pieces, gate, up):
    dim, width = gate.shape
    tokens = 4 * pieces[0].shape[0]
    tile = min(256, width)
    return call(
        "ffn_gate",
        gate_body,
        width // tile,
        [whole(p) for p in pieces] + [columns(gate, tile), columns(up, tile)],
        [new_columns(tokens, width, tile)] * 3,
        [*pieces, gate, up],
        4 * tokens * dim * width,
        weight=20.0,
    )


def ffn_slope_body(*refs):
    pieces, (w, silu, slope, dgate, dup) = refs[:4], refs[4:]
    rows = pieces[0].shape[0]
    for i in range(4):
        at = pl.ds(i * rows, rows)
        dact = dot(pieces[i][...], w[...], NN)
        dgate[at] = (dact * slope[at].astype(F32)).astype(BF)
        dup[at] = (dact * silu[at].astype(F32)).astype(BF)


def ffn_slope(pieces, down, silu, slope):
    dim, width = down.shape
    tokens = 4 * pieces[0].shape[0]
    tile = min(512, width)
    return call(
        "ffn_slope",
        ffn_slope_body,
        width // tile,
        [whole(p) for p in pieces] + [columns(a, tile) for a in (down, silu, slope)],
        [new_columns(tokens, width, tile)] * 2,
        [*pieces, down, silu, slope],
        2 * tokens * dim * width,
    )


def transposed_dot(left, b, columns):
    rows = left[0].shape[0]
    total = None
    for i in range(4):
        term = dot(left[i][:, columns], b[i * rows : (i + 1) * rows], TN)
        total = term if total is None else total + term
    return total.astype(BF)


def weight_grad(pieces, b, into=None):
    rows, dim = pieces[0].shape
    width = b.shape[1]
    tile = next(t for t in (512, 384, 256) if width % t == 0)
    step = min(512, dim)
    into = [] if into is None else [into]

    def body(*refs):
        for d in range(0, dim, step):
            refs[-1][d : d + step] = transposed_dot(refs[:4], refs[4], slice(d, d + step))

    return call(
        "weight_grad",
        body,
        width // tile,
        [whole(p) for p in pieces] + [columns(b, tile)] + [None] * len(into),
        [new_columns(dim, into[0].shape[1] if into else width, tile)],
        [*pieces, b, *into],
        8 * rows * dim * width,
        aliases={5: 0} if into else None,
    )[0]


def back(acts, weights, pieces, tile, sums=None, weight=1.0):
    rows = acts[0].shape[0] // 4
    dim = weights[0][0].shape[0]
    tile = min(tile, dim)
    na, np_ = len(acts), len(pieces)
    extra = [] if sums is None else [sums[p] for p in pieces]

    def body(*refs):
        ws = refs[na * np_ : na * np_ + na]
        outs = refs[na * np_ + na + len(extra) :]
        summed = None
        for p in range(np_):
            total = None
            for a in range(na):
                term = dot(refs[p * na + a][...], ws[a][...], NT)
                total = term if total is None else total + term
            outs[p][...] = total.astype(BF)
            if extra:
                term = total * refs[na * np_ + na + p][...].astype(F32)
                term = jnp.sum(term, axis=0, keepdims=True)
                summed = term if summed is None else summed + term
        if extra:
            outs[np_][...] = summed

    return call(
        "back",
        body,
        dim // tile,
        [((rows, a.shape[1]), lambda j, p=p: (p, 0), "held") for p in pieces for a in acts]
        + [((tile, a.shape[1]), lambda j, c=c: (j, c)) for a, (_, c) in zip(acts, weights)]
        + [columns(v, tile) for v in extra],
        [new_columns(rows, dim, tile)] * np_
        + ([new_columns(1, dim, tile, F32)] if extra else []),
        [a for _ in pieces for a in acts] + [w for w, _ in weights] + extra,
        2 * np_ * rows * dim * sum(a.shape[1] for a in acts),
        weight=weight,
    )


def shifted(ref, place, near, seg, back_way):
    cur = ref[place * seg : (place + 1) * seg]
    row = jnp.maximum(near, 0) * seg + (0 if back_way else seg - 8)
    edge = ref[pl.ds(pl.multiple_of(row, 8), 8)]
    edge = jnp.where(near >= 0, edge, 0.0)
    return jnp.concatenate([cur, edge] if back_way else [edge, cur])


def conv_of(ref, place, near, seg, taps):
    ext = shifted(ref, place, near, seg, False)
    terms = [ext[6 : 6 + seg], ext[7 : 7 + seg], ext[8 : 8 + seg]]
    return taps[0] * terms[0] + taps[1] * terms[1] + taps[2] * terms[2], terms


def conv_body(places, *refs):
    pieces, (w, taps_ref, bgate, cgate, xgate, ygate, mixed) = refs[:4], refs[4:]
    rows = pieces[0].shape[0]
    tile = bgate.shape[1]
    for i in range(4):
        at = pl.ds(i * rows, rows)
        b = dot(pieces[i][...], w[:, :tile], NN)
        x = dot(pieces[i][...], w[:, 2 * tile :], NN)
        c = dot(pieces[i][...], w[:, tile : 2 * tile], NN)
        mixed[at] = b * x
        bgate[at] = b.astype(BF)
        cgate[at] = c.astype(BF)
        xgate[at] = x.astype(BF)
    taps = [taps_ref[k : k + 1] for k in range(3)]
    segs = places.shape[1]
    seg = mixed.shape[0] // segs
    for s in range(segs):
        conv, _ = conv_of(mixed, s, places[0, s], seg, taps)
        at = pl.ds(s * seg, seg)
        ygate[at] = (cgate[at].astype(F32) * conv).astype(BF)


def conv_forward(pieces, weights, taps, places, tile):
    chans = taps.shape[1]
    dim = weights.shape[0]
    tokens = 4 * pieces[0].shape[0]
    return call(
        "conv_fwd",
        conv_body,
        chans // tile,
        [whole(p) for p in pieces]
        + [((dim, 3 * tile), lambda j: (0, j)), ((3, tile), lambda j: (0, j))],
        [new_columns(tokens, chans, tile)] * 4,
        [*pieces, weights, taps],
        6 * tokens * dim * chans,
        [pltpu.VMEM((tokens, tile), F32)],
        [places],
    )


def conv_back_body(places, *refs):
    pieces = refs[:4]
    w, taps_ref, bgate, cgate, xgate, ygate, dproj, tap_grad, out_grad, mixed, dconv = refs[4:]
    taps = [taps_ref[k : k + 1] for k in range(3)]
    segs = places.shape[1]
    tokens, tile = mixed.shape
    seg = tokens // segs
    mixed[...] = bgate[...].astype(F32) * xgate[...].astype(F32)
    rows = pieces[0].shape[0]
    sums = [jnp.zeros((1, tile), F32) for _ in range(3)]
    for i in range(4):
        dy = dot(pieces[i][...], w[...], NN)
        for s in range(i * segs // 4, (i + 1) * segs // 4):
            at = pl.ds(s * seg, seg)
            low = s * seg - i * rows
            dys = dy[low : low + seg]
            conv, terms = conv_of(mixed, s, places[0, s], seg, taps)
            dc = dys * cgate[at].astype(F32)
            dconv[at] = dc
            dproj[at, tile : 2 * tile] = (dys * conv).astype(BF)
            sums = [v + jnp.sum(dc * term, axis=0, keepdims=True) for v, term in zip(sums, terms)]
    for k in range(3):
        tap_grad[k : k + 1] = sums[k]
    for s in range(segs):
        at = pl.ds(s * seg, seg)
        ext = shifted(dconv, s, places[1, s], seg, True)
        dbx = taps[2] * ext[:seg] + taps[1] * ext[1 : 1 + seg] + taps[0] * ext[2 : 2 + seg]
        dproj[at, :tile] = (dbx * xgate[at].astype(F32)).astype(BF)
        dproj[at, 2 * tile :] = (dbx * bgate[at].astype(F32)).astype(BF)
    dim = pieces[0].shape[1]
    for d in range(0, dim, 512):
        out_grad[d : d + 512] = transposed_dot(pieces, ygate, slice(d, d + 512))


def conv_backward(pieces, weights, taps, saved, places, tile):
    chans = taps.shape[1]
    dim = weights.shape[0]
    tokens = 4 * pieces[0].shape[0]
    return call(
        "conv_bwd",
        conv_back_body,
        chans // tile,
        [whole(p) for p in pieces]
        + [columns(weights, tile, 3 * chans // tile), ((3, tile), lambda j: (0, j))]
        + [columns(a, tile) for a in saved],
        [
            ((tokens, 3 * tile), lambda j: (0, j), (tokens, 3 * chans), BF),
            ((3, tile), lambda j: (0, j), (3, chans), F32),
            ((dim, tile), lambda j: (0, 3 * chans // tile + j), (dim, 4 * chans), BF),
        ],
        [*pieces, weights, taps, *saved],
        4 * tokens * dim * chans,
        [pltpu.VMEM((tokens, tile), F32)] * 2,
        [places],
        weight=88.0,
    )


def local(
    sizes,
    tokens,
    in_weight,
    conv_taps,
    out_weight,
    gate_weight,
    up_weight,
    down_weight,
    norm_gain1,
    norm_gain2,
    out_grad,
):
    ndp, nt = sizes
    square = Square(nt)
    chans, dim = out_weight.shape[0], tokens.shape[2]
    offset = square.t * chans
    tile = min(256, chans)
    places = square.places()
    taps = lax.dynamic_slice_in_dim(conv_taps, offset, chans, 1)
    dp_gather = lambda v: lax.all_gather(v, "dp", axis=0, tiled=True)
    dp_scatter = lambda v: lax.psum_scatter(v, "dp", scatter_dimension=0, tiled=True)

    conv_shard = pack(in_weight, out_weight, tile)
    conv_w = dp_gather(conv_shard)
    down_shard = down_weight.T

    hidden = tokens[0].astype(F32)
    scale1 = rms_scale(hidden)
    cot = out_grad[0]
    g_gather = square.gather_steps(cot)
    g_one, _ = next(g_gather)
    n1, _ = square.gather((hidden * scale1 * norm_gain1).astype(BF), *g_one)
    gate_w = dp_gather(after(gate_weight, conv_w, n1[1], n1[3]))
    g_two, g_first = g_gather.send((n1[1], n1[3]))
    saved = conv_forward(n1, conv_w, taps, places, tile)
    ygate = saved[3]
    far = back([after(ygate, *g_first)], [(conv_w, 3)], (1, 3), 1024)
    near = back([after(ygate, far[0])], [(conv_w, 3)], (0, 2), 1024)
    branch, mid, _ = square.finish(near, square.begin(far), *g_two)
    up_w = dp_gather(after(up_weight, gate_w, *mid))
    second = hidden + branch
    scale2 = rms_scale(second)
    n2, n2_first = square.gather((second * scale2 * norm_gain2).astype(BF))
    down_w = dp_gather(after(down_shard, up_w, *n2_first))
    while g_first:
        g_two, g_first = g_gather.send((n2[1], n2[3]))
    g = g_two

    act, silu, slope = ffn_gate(n2, gate_w, up_w)
    down_part = weight_grad(first_after(g, act), act)
    down_owned = dp_scatter(down_part)
    dgate, dup = ffn_slope(first_after(g, down_part), down_w, silu, slope)
    pair = [(gate_w, 0), (up_w, 0)]
    far = back([dgate, dup], pair, (1, 3), 512)
    near = back([after(dgate, far[0]), dup], pair, (0, 2), 512)
    gate_part = weight_grad(first_after(n2, near[0]), dgate)
    dnormed2, mid, _ = square.finish(near, square.begin(far), gate_part)
    gate_owned = dp_scatter(after(gate_part, down_owned, *mid))
    ffn = back([after(act, *mid)], [(down_w, 0)], (1, 3, 0, 2), 512)
    dsecond_norm, gain2_part = norm_back(second, scale2, norm_gain2, dnormed2)
    dsecond = cot.astype(F32) + dsecond_norm
    sent = after(dsecond.astype(BF), ffn[0])
    dbr, dbr_first = square.gather(sent)
    up_part = weight_grad(first_after(n2, sent), dup)
    up_owned = dp_scatter(after(up_part, gate_owned, *dbr_first))

    dproj, tap_part, conv_part = conv_backward(
        first_after(dbr, up_part), conv_w, taps, saved, places, tile
    )
    came = square.begin([after(v, dbr[1], dbr[3]) for v in ffn[:2]])
    far = back([dproj], [(conv_w, 0)], (1, 3), 512, n1)
    conv_part = weight_grad(first_after(n1, far[0], *came), dproj, conv_part)
    ffn, ffn_sends, _ = square.finish(ffn[2:], came)
    near = back([after(dproj, conv_part, *ffn_sends)], [(conv_w, 0)], (0, 2), 512, n1, 150.0)
    first_came = square.begin(far[:2])
    dnormed, mid, last_came = square.finish(near[:2], first_came)
    conv_owned = dp_scatter(after(conv_part, up_owned))
    gain1_part = (far[2] + near[2])[0] / norm_gain1
    block_out = (second + ffn).astype(BF)
    dhidden_norm, _ = norm_back(hidden, scale1, norm_gain1, dnormed)
    tokens_grad = dsecond + dhidden_norm

    wide = lax.dynamic_update_slice_in_dim(
        jnp.zeros((3, conv_taps.shape[1]), F32), tap_part, offset, 1
    )
    small = jnp.concatenate(
        [gain1_part[None], gain2_part[None], wide, jnp.zeros_like(wide)]
    )
    small = total_of(after(small, *first_came), "dp", ndp)
    small = total_of(after(small, *last_came), "tensor", nt)
    in_owned, out_owned = unpack(conv_owned, chans, tile)
    return (
        block_out[None],
        tokens_grad[None],
        in_owned,
        small[2:5],
        out_owned,
        gate_owned.astype(F32),
        up_owned.astype(F32),
        down_owned.T.astype(F32),
        small[0],
        small[1],
    )


def solution(mesh):
    in_specs = (
        P("dp", "tensor", None),
        P(None, "dp", "tensor"),
        P(),
        P("tensor", "dp"),
        P("dp", "tensor"),
        P("dp", "tensor"),
        P("tensor", "dp"),
        P(),
        P(),
        P("dp", "tensor", None),
    )
    out_specs = (
        P("dp", "tensor", None),
        P("dp", "tensor", None),
        P(None, "dp", "tensor"),
        P(),
        P("tensor", "dp"),
        P("dp", "tensor"),
        P("dp", "tensor"),
        P("tensor", "dp"),
        P(),
        P(),
    )
    sizes = (mesh.shape["dp"], mesh.shape["tensor"])
    return jax.shard_map(
        functools.partial(local, sizes),
        mesh=mesh,
        in_specs=in_specs,
        out_specs=out_specs,
        check_vma=False,
    )
```

```python
import functools
import math

import jax
import jax.numpy as jnp
import numpy as np
from jax import lax
from jax.experimental import pallas as pl
from jax.experimental.pallas import tpu as pltpu
from jax.sharding import PartitionSpec as P

EPS = 1e-05
BF = jnp.bfloat16
F32 = jnp.float32
VMEM_LIMIT = 58 * 2**20
COST = 0.2
NN = (((1,), (0,)), ((), ()))
NT = (((1,), (1,)), ((), ()))
TN = (((0,), (0,)), ((), ()))


def dot(a, b, dims):
    return lax.dot_general(a, b, dims, preferred_element_type=F32)


def after(value, *others):
    if not others:
        return value
    return lax.optimization_barrier((value, others))[0]


def first_after(pieces, *others):
    return [after(pieces[0], *others)] + list(pieces[1:])


def rms_scale(values):
    return lax.rsqrt(jnp.mean(values * values, axis=-1, keepdims=True) + EPS)


def norm_back(hidden, scale, gain, grad):
    scaled = gain * grad
    back = scale * scaled - hidden * scale**3 * jnp.mean(scaled * hidden, axis=-1, keepdims=True)
    return back, jnp.sum(grad * hidden * scale, axis=0)


class Square:
    def __init__(self, nt):
        self.nt = nt
        self.t = lax.axis_index("tensor")
        bits = [1 << i for i in range(int(math.log2(nt)))]
        self.orders = (bits, bits[::-1])
        self.lists = []
        for order in self.orders:
            seen = [0]
            for bit in order:
                seen = seen + [r ^ bit for r in seen]
            self.lists.append(seen)

    def flip(self, value, bit):
        return lax.ppermute(value, "tensor", [(t, t ^ bit) for t in range(self.nt)])

    def gather(self, rows, *gates):
        half = rows.shape[0] // 2
        curs = [rows[:half], rows[half:]]
        depth = len(self.orders[0])
        first = None
        for level in range(depth):
            came = [self.flip(c, o[level]) for c, o in zip(curs, self.orders)]
            first = first or came
            if level < depth - 1:
                curs = [after(jnp.concatenate([c, r]), *gates) for c, r in zip(curs, came)]
        return [curs[0], came[0], curs[1], came[1]], first

    def gather_steps(self, rows):
        half = rows.shape[0] // 2
        curs = [rows[:half], rows[half:]]
        depth = len(self.orders[0])
        came = None
        for level in range(depth):
            gates = yield curs, came
            curs = [after(c, *gates) for c in curs]
            came = [self.flip(c, o[level]) for c, o in zip(curs, self.orders)]
            if level < depth - 1:
                curs = [jnp.concatenate([c, r]) for c, r in zip(curs, came)]
        yield [curs[0], came[0], curs[1], came[1]], None

    def begin(self, far):
        return [self.flip(s, o[-1]) for s, o in zip(far, self.orders)]

    def finish(self, near, came, *gates):
        depth = len(self.orders[0])
        total = lambda terms: sum(v.astype(F32) for v in terms)
        parts = [[k, r] for k, r in zip(near, came)]
        sends = came
        for level in range(depth - 1, 0, -1):
            half = parts[0][0].shape[0] // 2
            sends = [after(total([v[half:] for v in p]).astype(BF), *gates) for p in parts]
            came = [self.flip(s, o[level - 1]) for s, o in zip(sends, self.orders)]
            parts = [[v[:half] for v in p] + [r] for p, r in zip(parts, came)]
        return jnp.concatenate([total(p) for p in parts]), sends, came

    def places(self):
        index = {}
        for h, seen in enumerate(self.lists):
            for i, r in enumerate(seen):
                index[r, h] = h * self.nt + i
        table = np.zeros((self.nt, 2, 2 * self.nt), np.int32)
        for t in range(self.nt):
            for (r, h), i in index.items():
                at = t ^ r
                if h:
                    table[t, 0, i] = index[r, 0]
                    table[t, 1, i] = -1 if at == self.nt - 1 else index[(at + 1) ^ t, 0]
                else:
                    table[t, 0, i] = -1 if at == 0 else index[(at - 1) ^ t, 1]
                    table[t, 1, i] = index[r, 1]
        return lax.dynamic_index_in_dim(jnp.asarray(table), self.t, keepdims=False)


def total_of(value, axis, size):
    bit = 1
    while bit < size:
        value = value + lax.ppermute(value, axis, [(i, i ^ bit) for i in range(size)])
        bit *= 2
    return value


def call(name, body, grid, ins, outs, args, flops, scratch=(), scalars=(), aliases=None, weight=1.0):
    held = lambda spec: pl.BlockSpec(memory_space=pl.ANY) if spec is None else pl.BlockSpec(
        spec[0],
        lambda j, *_: spec[1](j),
        **({"pipeline_mode": pl.Buffered(1)} if len(spec) > 2 and spec[2] == "held" else {}),
    )
    moved = sum(math.prod(a.shape) * a.dtype.itemsize for a in args)
    moved += sum(math.prod(o[2]) * jnp.dtype(o[3]).itemsize for o in outs)
    return pl.pallas_call(
        body,
        grid_spec=pltpu.PrefetchScalarGridSpec(
            num_scalar_prefetch=len(scalars),
            grid=(grid,),
            in_specs=[held(s) for s in ins],
            out_specs=[pl.BlockSpec(o[0], lambda j, *_, o=o: o[1](j)) for o in outs],
            scratch_shapes=list(scratch),
        ),
        out_shape=[jax.ShapeDtypeStruct(o[2], o[3]) for o in outs],
        name=name,
        input_output_aliases=aliases or {},
        compiler_params=pltpu.CompilerParams(vmem_limit_bytes=VMEM_LIMIT),
        cost_estimate=pl.CostEstimate(
            flops=int(flops * COST * weight),
            bytes_accessed=int(moved * COST * weight),
            transcendentals=0,
        ),
    )(*scalars, *args)


def whole(a):
    return (a.shape, lambda j: (0,) * a.ndim, "held")


def columns(a, tile, start=0):
    return ((a.shape[0], tile), lambda j: (0, start + j))


def new_columns(rows, width, tile, dtype=BF):
    return ((rows, tile), lambda j: (0, j), (rows, width), dtype)


def pack(in_weight, out_weight, tile):
    kinds, depth, chans = in_weight.shape

    def body(win, wout, packed):
        for j in range(chans // tile):
            for k in range(kinds):
                at = (j * kinds + k) * tile
                packed[:, at : at + tile] = win[k, :, j * tile : (j + 1) * tile]
        packed[:, kinds * chans :] = wout[...].astype(F32).T.astype(BF)

    width = (kinds + 1) * chans
    return call(
        "pack",
        body,
        1,
        [whole(in_weight), whole(out_weight)],
        [new_columns(depth, width, width)],
        [in_weight, out_weight],
        0,
    )[0]


def unpack(packed, chans, tile):
    depth = packed.shape[0]
    kinds = packed.shape[1] // chans - 1

    def body(src, win, wout):
        for j in range(chans // tile):
            for k in range(kinds):
                at = (j * kinds + k) * tile
                win[k, :, j * tile : (j + 1) * tile] = src[:, at : at + tile].astype(F32)
        wout[...] = src[:, kinds * chans :].astype(F32).T

    return call(
        "unpack",
        body,
        1,
        [whole(packed)],
        [
            ((kinds, depth, chans), lambda j: (0, 0, 0), (kinds, depth, chans), F32),
            ((chans, depth), lambda j: (0, 0), (chans, depth), F32),
        ],
        [packed],
        0,
    )


def gate_body(*refs):
    pieces, (gw, uw) = refs[:2], refs[2:4]
    act, silu, slope = refs[-3:]
    for i in range(2):

        @pl.when(pl.program_id(0) % 2 == i)
        def _():
            gate = dot(pieces[i][...], gw[...], NN)
            up = dot(pieces[i][...], uw[...], NN)
            sig = jax.nn.sigmoid(gate)
            s = gate * sig
            act[...] = (s * up).astype(BF)
            silu[...] = s.astype(BF)
            slope[...] = (up * sig * (1.0 + gate * (1.0 - sig))).astype(BF)


def ffn_gate(pieces, gate, up, first, weight, into=()):
    rows, dim = pieces[0].shape
    width = gate.shape[1]
    tile = min(256, width)
    wspec = ((dim, tile), lambda j: (0, j // 2))
    out = ((rows, tile), lambda j: (first + 2 * (j % 2), j // 2), (4 * rows, width), BF)
    return call(
        "ffn_gate",
        gate_body,
        2 * width // tile,
        [whole(p) for p in pieces] + [wspec, wspec] + [None] * len(into),
        [out] * 3,
        [*pieces, gate, up, *into],
        8 * rows * dim * width,
        aliases={4 + i: i for i in range(len(into))},
        weight=weight,
    )


def ffn_slope_body(*refs):
    pieces, (w, silu, slope, dgate, dup) = refs[:4], refs[4:]
    rows = pieces[0].shape[0]
    for i in range(4):
        at = pl.ds(i * rows, rows)
        dact = dot(pieces[i][...], w[...], NN)
        dgate[at] = (dact * slope[at].astype(F32)).astype(BF)
        dup[at] = (dact * silu[at].astype(F32)).astype(BF)


def ffn_slope(pieces, down, silu, slope):
    dim, width = down.shape
    tokens = 4 * pieces[0].shape[0]
    tile = min(512, width)
    return call(
        "ffn_slope",
        ffn_slope_body,
        width // tile,
        [whole(p) for p in pieces] + [columns(a, tile) for a in (down, silu, slope)],
        [new_columns(tokens, width, tile)] * 2,
        [*pieces, down, silu, slope],
        2 * tokens * dim * width,
    )


def transposed_dot(left, b, columns):
    rows = left[0].shape[0]
    total = None
    for i in range(4):
        term = dot(left[i][:, columns], b[i * rows : (i + 1) * rows], TN)
        total = term if total is None else total + term
    return total.astype(BF)


def part_grad(pieces, b, which, prior=()):
    rows, dim = pieces[0].shape
    width = b.shape[1]
    tile = next(t for t in (512, 384, 256) if width % t == 0)
    step = min(512, dim)

    def body(*refs):
        for d in range(0, dim, step):
            total = None
            for ref, p in zip(refs[:2], which):
                term = dot(ref[:, d : d + step], refs[2][p * rows : (p + 1) * rows], TN)
                total = term if total is None else total + term
            if prior:
                total = total + refs[3][d : d + step].astype(F32)
            refs[-1][d : d + step] = total.astype(BF)

    return call(
        "part_grad",
        body,
        width // tile,
        [whole(p) for p in pieces] + [columns(v, tile) for v in (b, *prior)],
        [new_columns(dim, width, tile)],
        [*pieces, b, *prior],
        4 * rows * dim * width,
    )[0]


def weight_grad(pieces, b, into=None):
    rows, dim = pieces[0].shape
    width = b.shape[1]
    tile = next(t for t in (512, 384, 256) if width % t == 0)
    step = min(512, dim)
    into = [] if into is None else [into]

    def body(*refs):
        for d in range(0, dim, step):
            refs[-1][d : d + step] = transposed_dot(refs[:4], refs[4], slice(d, d + step))

    return call(
        "weight_grad",
        body,
        width // tile,
        [whole(p) for p in pieces] + [columns(b, tile)] + [None] * len(into),
        [new_columns(dim, into[0].shape[1] if into else width, tile)],
        [*pieces, b, *into],
        8 * rows * dim * width,
        aliases={5: 0} if into else None,
    )[0]


def back(acts, weights, pieces, tile, sums=None, weight=1.0):
    rows = acts[0].shape[0] // 4
    dim = weights[0][0].shape[0]
    tile = min(tile, dim)
    na, np_ = len(acts), len(pieces)
    extra = [] if sums is None else [sums[p] for p in pieces]

    def body(*refs):
        ws = refs[na * np_ : na * np_ + na]
        outs = refs[na * np_ + na + len(extra) :]
        summed = None
        for p in range(np_):
            total = None
            for a in range(na):
                term = dot(refs[p * na + a][...], ws[a][...], NT)
                total = term if total is None else total + term
            outs[p][...] = total.astype(BF)
            if extra:
                term = total * refs[na * np_ + na + p][...].astype(F32)
                term = jnp.sum(term, axis=0, keepdims=True)
                summed = term if summed is None else summed + term
        if extra:
            outs[np_][...] = summed

    return call(
        "back",
        body,
        dim // tile,
        [((rows, a.shape[1]), lambda j, p=p: (p, 0), "held") for p in pieces for a in acts]
        + [((tile, a.shape[1]), lambda j, c=c: (j, c)) for a, (_, c) in zip(acts, weights)]
        + [columns(v, tile) for v in extra],
        [new_columns(rows, dim, tile)] * np_
        + ([new_columns(1, dim, tile, F32)] if extra else []),
        [a for _ in pieces for a in acts] + [w for w, _ in weights] + extra,
        2 * np_ * rows * dim * sum(a.shape[1] for a in acts),
        weight=weight,
    )


def shifted(ref, place, near, seg, back_way):
    cur = ref[place * seg : (place + 1) * seg]
    row = jnp.maximum(near, 0) * seg + (0 if back_way else seg - 8)
    edge = ref[pl.ds(pl.multiple_of(row, 8), 8)]
    edge = jnp.where(near >= 0, edge, 0.0)
    return jnp.concatenate([cur, edge] if back_way else [edge, cur])


def conv_of(ref, place, near, seg, taps):
    ext = shifted(ref, place, near, seg, False)
    terms = [ext[6 : 6 + seg], ext[7 : 7 + seg], ext[8 : 8 + seg]]
    return taps[0] * terms[0] + taps[1] * terms[1] + taps[2] * terms[2], terms


def conv_body(places, *refs):
    pieces, (w, taps_ref, bgate, cgate, xgate, ygate, mixed) = refs[:4], refs[4:]
    rows = pieces[0].shape[0]
    tile = bgate.shape[1]
    for i in range(4):
        at = pl.ds(i * rows, rows)
        b = dot(pieces[i][...], w[:, :tile], NN)
        x = dot(pieces[i][...], w[:, 2 * tile :], NN)
        c = dot(pieces[i][...], w[:, tile : 2 * tile], NN)
        mixed[at] = b * x
        bgate[at] = b.astype(BF)
        cgate[at] = c.astype(BF)
        xgate[at] = x.astype(BF)
    taps = [taps_ref[k : k + 1] for k in range(3)]
    segs = places.shape[1]
    seg = mixed.shape[0] // segs
    for s in range(segs):
        conv, _ = conv_of(mixed, s, places[0, s], seg, taps)
        at = pl.ds(s * seg, seg)
        ygate[at] = (cgate[at].astype(F32) * conv).astype(BF)


def conv_forward(pieces, weights, taps, places, tile):
    chans = taps.shape[1]
    dim = weights.shape[0]
    tokens = 4 * pieces[0].shape[0]
    return call(
        "conv_fwd",
        conv_body,
        chans // tile,
        [whole(p) for p in pieces]
        + [((dim, 3 * tile), lambda j: (0, j)), ((3, tile), lambda j: (0, j))],
        [new_columns(tokens, chans, tile)] * 4,
        [*pieces, weights, taps],
        6 * tokens * dim * chans,
        [pltpu.VMEM((tokens, tile), F32)],
        [places],
    )


def conv_back_body(places, *refs):
    pieces = refs[:4]
    w, taps_ref, bgate, cgate, xgate, ygate, dproj, tap_grad, out_grad, mixed, dconv = refs[4:]
    taps = [taps_ref[k : k + 1] for k in range(3)]
    segs = places.shape[1]
    tokens, tile = mixed.shape
    seg = tokens // segs
    mixed[...] = bgate[...].astype(F32) * xgate[...].astype(F32)
    rows = pieces[0].shape[0]
    sums = [jnp.zeros((1, tile), F32) for _ in range(3)]
    for i in range(4):
        dy = dot(pieces[i][...], w[...], NN)
        for s in range(i * segs // 4, (i + 1) * segs // 4):
            at = pl.ds(s * seg, seg)
            low = s * seg - i * rows
            dys = dy[low : low + seg]
            conv, terms = conv_of(mixed, s, places[0, s], seg, taps)
            dc = dys * cgate[at].astype(F32)
            dconv[at] = dc
            dproj[at, tile : 2 * tile] = (dys * conv).astype(BF)
            sums = [v + jnp.sum(dc * term, axis=0, keepdims=True) for v, term in zip(sums, terms)]
    for k in range(3):
        tap_grad[k : k + 1] = sums[k]
    for s in range(segs):
        at = pl.ds(s * seg, seg)
        ext = shifted(dconv, s, places[1, s], seg, True)
        dbx = taps[2] * ext[:seg] + taps[1] * ext[1 : 1 + seg] + taps[0] * ext[2 : 2 + seg]
        dproj[at, :tile] = (dbx * xgate[at].astype(F32)).astype(BF)
        dproj[at, 2 * tile :] = (dbx * bgate[at].astype(F32)).astype(BF)
    dim = pieces[0].shape[1]
    for d in range(0, dim, 512):
        out_grad[d : d + 512] = transposed_dot(pieces, ygate, slice(d, d + 512))


def conv_backward(pieces, weights, taps, saved, places, tile):
    chans = taps.shape[1]
    dim = weights.shape[0]
    tokens = 4 * pieces[0].shape[0]
    return call(
        "conv_bwd",
        conv_back_body,
        chans // tile,
        [whole(p) for p in pieces]
        + [columns(weights, tile, 3 * chans // tile), ((3, tile), lambda j: (0, j))]
        + [columns(a, tile) for a in saved],
        [
            ((tokens, 3 * tile), lambda j: (0, j), (tokens, 3 * chans), BF),
            ((3, tile), lambda j: (0, j), (3, chans), F32),
            ((dim, tile), lambda j: (0, 3 * chans // tile + j), (dim, 4 * chans), BF),
        ],
        [*pieces, weights, taps, *saved],
        4 * tokens * dim * chans,
        [pltpu.VMEM((tokens, tile), F32)] * 2,
        [places],
        weight=88.0,
    )


def local(
    sizes,
    tokens,
    in_weight,
    conv_taps,
    out_weight,
    gate_weight,
    up_weight,
    down_weight,
    norm_gain1,
    norm_gain2,
    out_grad,
):
    ndp, nt = sizes
    square = Square(nt)
    chans, dim = out_weight.shape[0], tokens.shape[2]
    offset = square.t * chans
    tile = min(256, chans)
    places = square.places()
    taps = lax.dynamic_slice_in_dim(conv_taps, offset, chans, 1)
    dp_gather = lambda v: lax.all_gather(v, "dp", axis=0, tiled=True)
    dp_scatter = lambda v: lax.psum_scatter(v, "dp", scatter_dimension=0, tiled=True)

    conv_shard = pack(in_weight, out_weight, tile)
    conv_w = dp_gather(conv_shard)
    down_shard = down_weight.T

    hidden = tokens[0].astype(F32)
    scale1 = rms_scale(hidden)
    cot = out_grad[0]
    g_gather = square.gather_steps(cot)
    g_one, _ = next(g_gather)
    n1, _ = square.gather((hidden * scale1 * norm_gain1).astype(BF), *g_one)
    gate_w = dp_gather(after(gate_weight, conv_w, n1[1], n1[3]))
    g_two, g_first = g_gather.send((n1[1], n1[3]))
    saved = conv_forward(n1, conv_w, taps, places, tile)
    ygate = saved[3]
    far = back([after(ygate, *g_first)], [(conv_w, 3)], (1, 3), 1024)
    near = back([after(ygate, far[0])], [(conv_w, 3)], (0, 2), 1024)
    branch, mid, _ = square.finish(near, square.begin(far), *g_two)
    up_w = dp_gather(after(up_weight, gate_w, *mid))
    second = hidden + branch
    scale2 = rms_scale(second)
    n2, n2_first = square.gather((second * scale2 * norm_gain2).astype(BF))
    down_w = dp_gather(after(down_shard, up_w, *n2_first))
    gated = ffn_gate([n2[0], n2[2]], gate_w, up_w, 0, 1.0)
    while g_first:
        g_two, g_first = g_gather.send((n2[1], n2[3], gated[0]))
    g = g_two

    act, silu, slope = ffn_gate([n2[1], n2[3]], gate_w, up_w, 1, 40.0, gated)
    down_part = part_grad([g[0], g[2]], act, (0, 2))
    down_part = part_grad([g[1], g[3]], act, (1, 3), [down_part])
    down_owned = dp_scatter(down_part)
    dgate, dup = ffn_slope(first_after(g, down_part), down_w, silu, slope)
    pair = [(gate_w, 0), (up_w, 0)]
    far = back([dgate, dup], pair, (1, 3), 512)
    near = back([after(dgate, far[0]), dup], pair, (0, 2), 512)
    gate_part = weight_grad(first_after(n2, near[0]), dgate)
    dnormed2, mid, _ = square.finish(near, square.begin(far), gate_part)
    gate_owned = dp_scatter(after(gate_part, down_owned, *mid))
    ffn = back([after(act, *mid)], [(down_w, 0)], (1, 3, 0, 2), 512)
    dsecond_norm, gain2_part = norm_back(second, scale2, norm_gain2, dnormed2)
    dsecond = cot.astype(F32) + dsecond_norm
    sent = after(dsecond.astype(BF), ffn[0])
    dbr, dbr_first = square.gather(sent)
    up_part = weight_grad(first_after(n2, sent), dup)
    up_owned = dp_scatter(after(up_part, gate_owned, *dbr_first))

    dproj, tap_part, conv_part = conv_backward(
        first_after(dbr, up_part), conv_w, taps, saved, places, tile
    )
    came = square.begin([after(v, dbr[1], dbr[3]) for v in ffn[:2]])
    far = back([dproj], [(conv_w, 0)], (1, 3), 512, n1)
    conv_part = weight_grad(first_after(n1, far[0], *came), dproj, conv_part)
    ffn, ffn_sends, _ = square.finish(ffn[2:], came)
    near = back([after(dproj, conv_part, *ffn_sends)], [(conv_w, 0)], (0, 2), 512, n1, 150.0)
    first_came = square.begin(far[:2])
    dnormed, mid, last_came = square.finish(near[:2], first_came)
    conv_owned = dp_scatter(after(conv_part, up_owned))
    gain1_part = (far[2] + near[2])[0] / norm_gain1
    block_out = (second + ffn).astype(BF)
    dhidden_norm, _ = norm_back(hidden, scale1, norm_gain1, dnormed)
    tokens_grad = dsecond + dhidden_norm

    wide = lax.dynamic_update_slice_in_dim(
        jnp.zeros((3, conv_taps.shape[1]), F32), tap_part, offset, 1
    )
    small = jnp.concatenate(
        [gain1_part[None], gain2_part[None], wide, jnp.zeros_like(wide)]
    )
    small = total_of(after(small, *first_came), "dp", ndp)
    small = total_of(after(small, *last_came), "tensor", nt)
    in_owned, out_owned = unpack(conv_owned, chans, tile)
    return (
        block_out[None],
        tokens_grad[None],
        in_owned,
        small[2:5],
        out_owned,
        gate_owned.astype(F32),
        up_owned.astype(F32),
        down_owned.T.astype(F32),
        small[0],
        small[1],
    )


def solution(mesh):
    in_specs = (
        P("dp", "tensor", None),
        P(None, "dp", "tensor"),
        P(),
        P("tensor", "dp"),
        P("dp", "tensor"),
        P("dp", "tensor"),
        P("tensor", "dp"),
        P(),
        P(),
        P("dp", "tensor", None),
    )
    out_specs = (
        P("dp", "tensor", None),
        P("dp", "tensor", None),
        P(None, "dp", "tensor"),
        P(),
        P("tensor", "dp"),
        P("dp", "tensor"),
        P("dp", "tensor"),
        P("tensor", "dp"),
        P(),
        P(),
    )
    sizes = (mesh.shape["dp"], mesh.shape["tensor"])
    return jax.shard_map(
        functools.partial(local, sizes),
        mesh=mesh,
        in_specs=in_specs,
        out_specs=out_specs,
        check_vma=False,
    )
```
